32 devices in a mesh: dp: 8 (over z, core), pack: 4 (over y, x).
Axes of the slice: x: 2, y: 2, z: 4, core: 2. Of those that a mesh axis runs over, the one named last changes fastest.
Arguments:
- images: bfloat16 [64, 1152], P(('dp', 'pack')), may hold values from -6 to 6
- captions: bfloat16 [128, 1152], P(('dp', 'pack')), may hold values from -6 to 6
- caption_owner: int32 [128], P(('dp', 'pack')), may hold values from 0 to 7, as said below
- caption_count: int32 [32], P(('dp', 'pack')), may hold values from 0 to 4, as said below
- log_scale: float32 [1], replicated, may hold values from 1.6 to 2.6
- bias: float32 [1], replicated, may hold values from -3 to 0
Outputs:
- row_loss: float32 [64], P(('dp', 'pack'))
- grad_images: float32 [64, 1152], P(('dp', 'pack'))
- grad_captions: float32 [128, 1152], P(('dp', 'pack'))
The draws below stay inside these ranges and needn't reach their ends.
Inputs may be any that keep to these rules, and one draw needn't show every extreme that they name: `caption_owner`: within each pair block, the filled slots of its 4 devices name every one of its 8 pairs exactly once; values in empty slots are arbitrary. `caption_count`: the counts of one pair block's devices sum to 8.
All inputs are finite; a program needn't handle non-finite values.
Results may differ from the reference program's by a relative error of at most 0.0043.
Values may be sent and summed in bfloat16 or wider, within the bound.
No kernel may reach another device: no remote copies, remote signals or barrier semaphores. Data moves between devices by JAX's collectives and lax.ppermute only.
A program may use at most 64 MiB of HBM per device.

```python
import jax
import jax.numpy as jnp
from jax import lax

D = 1152
PAIR_DEV = 2
SLOTS = 4
PAIRS = 64
N_DP = 8
N_PACK = 4


def packing_plan(key):
    group_rows = PAIR_DEV * N_PACK
    key_weight, key_big, key_perm, key_fill = jax.random.split(key, 4)
    biggest = jax.random.randint(key_big, (N_DP,), 0, N_PACK)
    device_ids = jnp.arange(N_PACK, dtype=jnp.int32)[None, :]
    is_big = device_ids == biggest[:, None]
    shares = jax.random.randint(key_weight, (N_DP, N_PACK), 2, 4)
    shares = jnp.where(is_big, 0, shares)
    remain = (N_PACK - 2) * PAIR_DEV
    counts = remain * shares // jnp.sum(shares, axis=1, keepdims=True)
    deficit = remain - jnp.sum(counts, axis=1, keepdims=True)
    ranked = device_ids - (device_ids > biggest[:, None]).astype(jnp.int32)
    counts = counts + jnp.where(jnp.logical_and(ranked < deficit, jnp.logical_not(is_big)), 1, 0)
    counts = jnp.where(is_big, 2 * PAIR_DEV, counts).astype(jnp.int32)
    offsets = jnp.cumsum(counts, axis=1) - counts
    perm_keys = jax.random.split(key_perm, N_DP)
    orders = jax.vmap(lambda one_key: jax.random.permutation(one_key, group_rows))(perm_keys).astype(jnp.int32)
    filler = jax.random.randint(key_fill, (N_DP, N_PACK, SLOTS), 0, group_rows)
    slot_ids = jnp.arange(SLOTS, dtype=jnp.int32)[None, None, :]
    places = offsets[:, :, None] + slot_ids
    filled = slot_ids < counts[:, :, None]
    places = jnp.clip(places, 0, group_rows - 1).reshape(N_DP, N_PACK * SLOTS)
    taken = jnp.take_along_axis(orders, places, axis=1).reshape(N_DP, N_PACK, SLOTS)
    owners = jnp.where(filled, taken, filler).astype(jnp.int32)
    return (owners.reshape(N_DP * N_PACK * SLOTS), counts.reshape(N_DP * N_PACK))


def draw_caption_owner(key, part):
    owners, counts = packing_plan(key)
    return owners


def draw_caption_count(key, part):
    owners, counts = packing_plan(key)
    return counts


def block_scale(stream_key, shape, pieces, smallest, top_value):
    loudness, own = 1.0, jax.random.fold_in(stream_key, 6)
    for axis_at, shards_of in pieces:
        steps = jnp.exp(jax.random.uniform(jax.random.fold_in(own, axis_at), (shards_of,), jnp.float32, smallest / len(pieces), top_value / len(pieces)))
        loudness = loudness * jnp.repeat(steps, shape[axis_at] // shards_of).reshape([-1 if axis == axis_at else 1 for axis in range(len(shape))])
    return loudness


def scatter_about(key, extent, width, bound, cuts=(), held_as=jnp.bfloat16):
    array = jax.random.normal(key, extent, jnp.float32) * width
    if len(cuts) > 0:
        array = block_scale(key, extent, cuts, -0.22, 0.18) * array
    return jnp.clip(array, min=-bound, max=bound).astype(held_as)


def setup_inputs(seed: int = 0) -> dict:
    streams_of = jax.random.split(jax.random.key(seed), 7)
    images = scatter_about(streams_of[0], (PAIRS, D), 1.0, 6.0, ((0, 32),))
    captions = scatter_about(streams_of[1], (N_DP * N_PACK * SLOTS, D), 1.0, 6.0, ((0, 32),))
    caption_owner = draw_caption_owner(jax.random.fold_in(streams_of[6], 71), 0)
    caption_count = draw_caption_count(jax.random.fold_in(streams_of[6], 71), 0)
    log_scale = jnp.clip(jax.random.uniform(streams_of[4], (1,), jnp.float32, 1.6, 2.6), 1.6, 2.6)
    bias = jnp.clip(jax.random.uniform(streams_of[5], (1,), jnp.float32, -3.0, 0.0), -3.0, 0.0)
    return {"images": images, "captions": captions, "caption_owner": caption_owner, "caption_count": caption_count, "log_scale": log_scale, "bias": bias}


eps = 1e-06

def normalize(block_rows):
    floats = block_rows.astype(jnp.float32)
    inverse = lax.rsqrt(lax.optimization_barrier(jnp.sum(floats * floats, axis=-1, keepdims=True)) + eps)
    return (floats * inverse, inverse)

def unnormalize(unit_rows, inverse, upstream):
    return inverse * (upstream - unit_rows * lax.optimization_barrier(jnp.sum(unit_rows * upstream, axis=-1, keepdims=True)))

def reference(images, captions, caption_owner, caption_count, log_scale, bias):
    group_rows = PAIR_DEV * N_PACK
    slot_ids = jnp.arange(N_DP * N_PACK * SLOTS, dtype=jnp.int32)
    device_ids = slot_ids // SLOTS
    filled = slot_ids % SLOTS < caption_count[device_ids]
    target = device_ids // N_PACK * group_rows + caption_owner
    target = jnp.where(filled, target, PAIRS).astype(jnp.int32)
    owned_texts = jax.ops.segment_sum(captions.astype(jnp.float32), target, num_segments=PAIRS + 1)[:PAIRS].astype(jnp.bfloat16)
    image_unit, image_inv = normalize(images)
    image16 = image_unit.astype(jnp.bfloat16)
    text_unit, text_inv = normalize(owned_texts)
    text16 = text_unit.astype(jnp.bfloat16)
    logit_scale = jnp.exp(log_scale[0])
    logit_shift = bias[0]
    columns = jnp.arange(PAIRS, dtype=jnp.int32)

    def block_step(running, block_index):
        block_rows = lax.dynamic_slice_in_dim(image16, block_index * group_rows, group_rows, 0)
        logits = logit_scale * jnp.dot(block_rows, text16.T, preferred_element_type=jnp.float32) + logit_shift
        row_ids = block_index * group_rows + jnp.arange(group_rows, dtype=jnp.int32)
        labels = jnp.where(row_ids[:, None] == columns[None, :], 1.0, -1.0).astype(jnp.float32)
        losses = lax.optimization_barrier(jnp.sum(jax.nn.softplus(-labels * logits), axis=1)) / PAIRS
        weights = (-labels * jax.nn.sigmoid(-labels * logits)).astype(jnp.bfloat16)
        grad_rows = logit_scale * jnp.dot(weights, text16, preferred_element_type=jnp.float32)
        text_term = lax.dot_general(weights, block_rows, (((0,), (0,)), ((), ())), preferred_element_type=jnp.float32)
        return (running + text_term, (losses, grad_rows))
    text_sum, (losses, grad_unit) = lax.scan(block_step, jnp.zeros((PAIRS, D), jnp.float32), jnp.arange(N_DP, dtype=jnp.int32))
    row_loss = losses.reshape(PAIRS)
    grad_images = unnormalize(image_unit, image_inv, grad_unit.reshape(PAIRS, D))
    grad_texts = unnormalize(text_unit, text_inv, logit_scale * text_sum)
    picked = grad_texts[jnp.minimum(target, PAIRS - 1)]
    grad_captions = jnp.where(filled[:, None], picked, 0.0).astype(jnp.float32)
    return (row_loss, grad_images, grad_captions)
```

```python
import functools

import jax
import jax.numpy as jnp
from jax import lax
from jax.experimental import pallas as pl
from jax.experimental.pallas import tpu as pltpu
from jax.sharding import Mesh
from jax.sharding import PartitionSpec as P

eps = 1e-06
ROWS = 8
CHUNK = 16


def unit_rows(rows):
    floats = rows.astype(jnp.float32)
    inverse = lax.rsqrt(jnp.sum(floats * floats, axis=-1, keepdims=True) + eps)
    return floats * inverse, inverse


def pack_kernel(images_ref, captions_ref, owner_ref, count_ref, sent_ref):
    slots, width = captions_ref.shape
    images, _ = unit_rows(images_ref[...])
    captions, _ = unit_rows(captions_ref[...])
    left = ROWS - images_ref.shape[0] - slots
    lanes = lax.broadcasted_iota(jnp.int32, (left, width), 1)
    codes = jnp.zeros((left, width), jnp.float32)
    for slot in range(slots):
        code = jnp.where(slot < count_ref[0], owner_ref[slot], -1).astype(jnp.float32)
        codes = jnp.where(lanes == slot, code, codes)
    block = jnp.concatenate([images, captions, codes], axis=0).astype(jnp.bfloat16)

    def put(receiver):
        sent_ref[pl.ds(receiver * ROWS, ROWS), :] = block

    receivers = sent_ref.shape[0] // ROWS
    if receivers <= 16:
        for receiver in range(receivers):
            put(receiver)
    else:
        pl.loop(0, receivers)(put)


def pair_kernel(
    chips,
    packers,
    where_ref,
    owner_ref,
    count_ref,
    scale_ref,
    bias_ref,
    images_ref,
    captions_ref,
    mine_ref,
    other_ref,
    loss_ref,
    grad_images_ref,
    grad_captions_ref,
):
    pair_rows = images_ref.shape[0]
    slots, width = captions_ref.shape
    group_rows = pair_rows * packers
    chip_me, core_me, pack_me = where_ref[0], where_ref[1], where_ref[2]
    cycle_me = chip_me * 2 + core_me
    me = cycle_me * packers + pack_me
    devices = chips * 2 * packers
    chunk_rows = CHUNK * ROWS
    logit_scale = jnp.exp(jnp.full((1, 1), scale_ref[0], jnp.float32))
    logit_shift = bias_ref[0]

    images, images_inv = unit_rows(images_ref[...])
    captions, captions_inv = unit_rows(captions_ref[...])
    filler = jnp.zeros((ROWS - pair_rows - slots, width), jnp.float32)
    own = jnp.concatenate([images, captions, filler], axis=0)
    own_inv = jnp.concatenate([images_inv, captions_inv, filler[:, :1]], axis=0)
    own16 = own.astype(jnp.bfloat16)

    own_at = lax.broadcasted_iota(jnp.int32, (ROWS, 1), 0)
    own_pair = jnp.where(own_at < pair_rows, me * pair_rows + own_at, -1)
    for slot in range(slots):
        pair = jnp.where(slot < count_ref[0], cycle_me * group_rows + owner_ref[slot], -1)
        own_pair = jnp.where(own_at == pair_rows + slot, pair, own_pair)
    own_is_image = own_at < pair_rows

    column = lax.broadcasted_iota(jnp.int32, (1, chunk_rows), 1)
    column_at = column % ROWS
    column_is_image = column_at < pair_rows
    column_is_slot = jnp.logical_and(column_at >= pair_rows, column_at < pair_rows + slots)
    spread = (
        lax.broadcasted_iota(jnp.int32, (128, chunk_rows), 0)
        == lax.broadcasted_iota(jnp.int32, (128, chunk_rows), 1) % ROWS - pair_rows
    ).astype(jnp.bfloat16)
    code_row = lax.broadcasted_iota(jnp.int32, (chunk_rows, chunk_rows), 0)
    code_column = lax.broadcasted_iota(jnp.int32, (chunk_rows, chunk_rows), 1)
    code_here = code_row == code_column // ROWS * ROWS + pair_rows + slots

    def one_chunk(rows_ref, core_from, chunk, totals):
        loss, upstream = totals
        rows = rows_ref[pl.ds(chunk * chunk_rows, chunk_rows), :]
        codes = jnp.dot(rows[:, :128], spread, preferred_element_type=jnp.float32)
        codes = jnp.sum(jnp.where(code_here, codes, 0.0), axis=0, keepdims=True).astype(jnp.int32)
        block = chunk * CHUNK + column // ROWS
        cycle_at = block // packers * 2 + core_from
        device = cycle_at * packers + block % packers
        column_pair = jnp.where(
            column_is_image,
            device * pair_rows + column_at,
            jnp.where(
                jnp.logical_and(column_is_slot, codes >= 0), cycle_at * group_rows + codes, -1
            ),
        )
        live = jnp.logical_and(
            jnp.logical_and(own_pair >= 0, column_pair >= 0), own_is_image != column_is_image
        )
        products = lax.dot_general(
            own16, rows, (((1,), (1,)), ((), ())), preferred_element_type=jnp.float32
        )
        logits = logit_scale * products + logit_shift
        signed = jnp.where(own_pair == column_pair, -logits, logits)
        small = jnp.exp(-jnp.abs(signed))
        softplus = jnp.maximum(signed, 0.0) + jnp.log1p(small)
        sigmoid = jnp.where(signed >= 0.0, 1.0, small) / (1.0 + small)
        loss = loss + jnp.sum(jnp.where(live, softplus, 0.0), axis=1, keepdims=True)
        weights = jnp.where(own_pair == column_pair, -sigmoid, sigmoid)
        weights = jnp.where(live, weights, 0.0).astype(jnp.bfloat16)
        upstream = upstream + jnp.dot(weights, rows, preferred_element_type=jnp.float32)
        return loss, upstream

    totals = (jnp.zeros((ROWS, 1), jnp.float32), jnp.zeros((ROWS, width), jnp.float32))
    for rows_ref, core_from in ((mine_ref, core_me), (other_ref, 1 - core_me)):
        work = functools.partial(one_chunk, rows_ref, core_from)
        chunks = devices // 2 // CHUNK
        totals = work(0, totals) if chunks == 1 else lax.fori_loop(0, chunks, work, totals)
    loss, upstream = totals

    upstream = logit_scale * upstream
    grads = own_inv * (upstream - own * jnp.sum(own * upstream, axis=-1, keepdims=True))
    loss = loss / (devices * pair_rows)
    lanes = lax.broadcasted_iota(jnp.int32, (1, pair_rows), 1)
    losses = jnp.zeros((1, pair_rows), jnp.float32)
    for row in range(pair_rows):
        losses = jnp.where(lanes == row, loss[row : row + 1, :], losses)
    loss_ref[...] = losses
    grad_images_ref[...] = grads[:pair_rows]
    grad_captions_ref[...] = jnp.where(own_pair >= 0, grads, 0.0)[pair_rows : pair_rows + slots]


def body(images, captions, caption_owner, caption_count, log_scale, bias):
    pair_rows, width = images.shape
    slots = captions.shape[0]
    packers = lax.axis_size("pack")
    chips = lax.axis_size("chip")
    receivers = chips * packers
    assert pair_rows + slots < ROWS and slots <= 128 and pair_rows * packers <= 256
    assert receivers % CHUNK == 0
    where = jnp.stack([lax.axis_index("chip"), lax.axis_index("core"), lax.axis_index("pack")])
    vmem = pl.BlockSpec(memory_space=pltpu.VMEM)
    smem = pl.BlockSpec(memory_space=pltpu.SMEM)
    sent = pl.pallas_call(
        pack_kernel,
        out_shape=jax.ShapeDtypeStruct((receivers * ROWS, width), jnp.bfloat16),
        in_specs=[vmem, vmem, smem, smem],
        out_specs=vmem,
    )(images, captions, caption_owner, caption_count)
    mine = lax.all_to_all(sent, ("chip", "pack"), split_axis=0, concat_axis=0, tiled=True)
    other = lax.ppermute(mine, "core", [(0, 1), (1, 0)])
    row_loss, grad_images, grad_captions = pl.pallas_call(
        functools.partial(pair_kernel, chips, packers),
        out_shape=(
            jax.ShapeDtypeStruct((1, pair_rows), jnp.float32),
            jax.ShapeDtypeStruct(images.shape, jnp.float32),
            jax.ShapeDtypeStruct(captions.shape, jnp.float32),
        ),
        in_specs=[smem] * 5 + [vmem] * 4,
        out_specs=(vmem, vmem, vmem),
        compiler_params=pltpu.CompilerParams(vmem_limit_bytes=32 * 1024 * 1024),
    )(where, caption_owner, caption_count, log_scale, bias, images, captions, mine, other)
    return row_loss.reshape(pair_rows), grad_images, grad_captions


def solution(mesh):
    cycles, packers = mesh.devices.shape
    split = Mesh(mesh.devices.reshape(cycles // 2, 2, packers), ("chip", "core", "pack"))
    rows = P(("chip", "core", "pack"))
    return jax.shard_map(
        body,
        mesh=split,
        in_specs=(rows, rows, rows, rows, P(), P()),
        out_specs=(rows, rows, rows),
        check_vma=False,
    )
```

```python
import functools

import jax
import jax.numpy as jnp
from jax import lax
from jax.experimental import pallas as pl
from jax.experimental.pallas import tpu as pltpu
from jax.sharding import Mesh
from jax.sharding import PartitionSpec as P

eps = 1e-06
ROWS = 8
CHUNK = 16
APART = {"chip": (2, 3, 1), "pack": (3, 1, 2)}


def unit_rows(rows):
    floats = rows.astype(jnp.float32)
    inverse = lax.rsqrt(jnp.sum(floats * floats, axis=-1, keepdims=True) + eps)
    return floats * inverse, inverse


def pack_kernel(images_ref, captions_ref, owner_ref, count_ref, sent_ref, own_ref, aside_ref):
    pair_rows = images_ref.shape[0]
    slots, width = captions_ref.shape
    owner = owner_ref[...].reshape(1, slots).astype(jnp.float32)
    count = count_ref[0]
    left = ROWS - pair_rows - slots
    images, images_inv = unit_rows(images_ref[...])
    captions, captions_inv = unit_rows(captions_ref[...])
    codes = [jnp.where(slot < count, owner[:, slot : slot + 1], -1.0) for slot in range(slots)]
    own = jnp.concatenate([images, captions, jnp.zeros((left, width), jnp.float32)], axis=0)
    own_ref[...] = own
    own_inv = jnp.concatenate([images_inv, captions_inv, jnp.zeros((left, 1), jnp.float32)], axis=0)
    rows = lax.broadcasted_iota(jnp.int32, (ROWS, 128), 0)
    lanes = lax.broadcasted_iota(jnp.int32, (ROWS, 128), 1)
    aside = jnp.where(lanes == 0, own_inv, 0.0)
    for slot in range(slots):
        aside = jnp.where(jnp.logical_and(lanes == 1, rows == pair_rows + slot), codes[slot], aside)
    aside_ref[...] = aside
    front = own[:, :128]
    for slot in range(slots):
        here = jnp.logical_and(lanes == slot, rows == pair_rows + slots)
        front = jnp.where(here, codes[slot], front)
    block = jnp.concatenate([front, own[:, 128:]], axis=1)
    sent_ref[...] = block.astype(jnp.bfloat16)


def pair_kernel(
    chips,
    packers,
    pair_rows,
    slots,
    scale_ref,
    bias_ref,
    own_ref,
    aside_ref,
    mine_ref,
    other_ref,
    loss_ref,
    grad_images_ref,
    grad_captions_ref,
):
    width = own_ref.shape[1]
    group_rows = pair_rows * packers
    chip_me, core_me, pack_me = lax.axis_index("chip"), lax.axis_index("core"), lax.axis_index("pack")
    cycle_me = chip_me * 2 + core_me
    me = cycle_me * packers + pack_me
    devices = chips * 2 * packers
    chunk_rows = CHUNK * ROWS

    own = own_ref[...]
    own16 = own.astype(jnp.bfloat16)
    aside = aside_ref[...]
    own_inv, own_codes = aside[:, 0:1], aside[:, 1:2].astype(jnp.int32)
    logit_scale = jnp.exp(jnp.full((1, 1), scale_ref[0], jnp.float32))
    logit_shift = bias_ref[0]

    own_at = lax.broadcasted_iota(jnp.int32, (ROWS, 1), 0)
    own_is_image = own_at < pair_rows
    own_is_slot = jnp.logical_and(own_at >= pair_rows, own_at < pair_rows + slots)
    own_pair = jnp.where(
        own_is_image,
        me * pair_rows + own_at,
        jnp.where(jnp.logical_and(own_is_slot, own_codes >= 0), cycle_me * group_rows + own_codes, -1),
    )

    column = lax.broadcasted_iota(jnp.int32, (1, chunk_rows), 1)
    column_at = column % ROWS
    column_is_image = column_at < pair_rows
    column_is_slot = jnp.logical_and(column_at >= pair_rows, column_at < pair_rows + slots)
    spread = (
        lax.broadcasted_iota(jnp.int32, (128, chunk_rows), 0)
        == lax.broadcasted_iota(jnp.int32, (128, chunk_rows), 1) % ROWS - pair_rows
    ).astype(jnp.bfloat16)
    code_row = lax.broadcasted_iota(jnp.int32, (chunk_rows, chunk_rows), 0)
    code_column = lax.broadcasted_iota(jnp.int32, (chunk_rows, chunk_rows), 1)
    code_here = code_row == code_column // ROWS * ROWS + pair_rows + slots

    def one_chunk(rows_ref, core_from, chunk, totals):
        loss, upstream = totals
        rows = rows_ref[pl.ds(chunk * chunk_rows, chunk_rows), :]
        codes = jnp.dot(rows[:, :128], spread, preferred_element_type=jnp.float32)
        codes = jnp.sum(jnp.where(code_here, codes, 0.0), axis=0, keepdims=True).astype(jnp.int32)
        block = chunk * CHUNK + column // ROWS
        chip_at, core_at, pack_at = source(block, chip_me, core_from, pack_me, chips, packers)
        cycle_at = chip_at * 2 + core_at
        device = cycle_at * packers + pack_at
        column_pair = jnp.where(
            column_is_image,
            device * pair_rows + column_at,
            jnp.where(
                jnp.logical_and(column_is_slot, codes >= 0), cycle_at * group_rows + codes, -1
            ),
        )
        live = jnp.logical_and(
            jnp.logical_and(own_pair >= 0, column_pair >= 0), own_is_image != column_is_image
        )
        products = lax.dot_general(
            own16, rows, (((1,), (1,)), ((), ())), preferred_element_type=jnp.float32
        )
        logits = logit_scale * products + logit_shift
        signed = jnp.where(own_pair == column_pair, -logits, logits)
        small = jnp.exp(-jnp.abs(signed))
        softplus = jnp.maximum(signed, 0.0) + jnp.log1p(small)
        sigmoid = jnp.where(signed >= 0.0, 1.0, small) / (1.0 + small)
        loss = loss + jnp.sum(jnp.where(live, softplus, 0.0), axis=1, keepdims=True)
        weights = jnp.where(own_pair == column_pair, -sigmoid, sigmoid)
        weights = jnp.where(live, weights, 0.0).astype(jnp.bfloat16)
        upstream = upstream + jnp.dot(weights, rows, preferred_element_type=jnp.float32)
        return loss, upstream

    totals = (jnp.zeros((ROWS, 1), jnp.float32), jnp.zeros((ROWS, width), jnp.float32))
    for rows_ref, core_from in ((mine_ref, core_me), (other_ref, 1 - core_me)):
        work = functools.partial(one_chunk, rows_ref, core_from)
        chunks = devices // 2 // CHUNK
        totals = work(0, totals) if chunks == 1 else lax.fori_loop(0, chunks, work, totals)
    loss, upstream = totals

    upstream = logit_scale * upstream
    grads = own_inv * (upstream - own * jnp.sum(own * upstream, axis=-1, keepdims=True))
    loss = loss / (devices * pair_rows)
    lanes = lax.broadcasted_iota(jnp.int32, (1, pair_rows), 1)
    losses = jnp.zeros((1, pair_rows), jnp.float32)
    for row in range(pair_rows):
        losses = jnp.where(lanes == row, loss[row : row + 1, :], losses)
    loss_ref[...] = losses
    grad_images_ref[...] = grads[:pair_rows]
    grad_captions_ref[...] = jnp.where(own_pair >= 0, grads, 0.0)[pair_rows : pair_rows + slots]


def gather(rows):
    chips, packers = lax.axis_size("chip"), lax.axis_size("pack")
    if chips != 4 or packers != 4:
        return lax.all_gather(lax.all_gather(rows, "chip", axis=0, tiled=True), "pack", axis=0, tiled=True)
    for axis, distances in APART.items():
        taken = [rows]
        for apart in distances:
            pairs = []
            for chip in range(4):
                for core in range(2):
                    for pack in range(4):
                        peer_chip = chip ^ apart if axis == "chip" else chip
                        peer_pack = pack ^ apart if axis == "pack" else pack
                        peer = (peer_chip * 2 + 1 - core) * 4 + peer_pack
                        pairs.append(((chip * 2 + core) * 4 + pack, peer))
            taken.append(lax.ppermute(rows, ("chip", "core", "pack"), pairs))
        rows = jnp.concatenate(taken, axis=0)
    return rows


def source(block, chip_me, core_me, pack_me, chips, packers):
    if chips != 4 or packers != 4:
        return block % chips, core_me, block // chips
    chip, core, pack = chip_me, core_me, pack_me
    for at, apart in enumerate(APART["chip"]):
        here = block % 4 == at + 1
        chip, core = jnp.where(here, chip_me ^ apart, chip), jnp.where(here, 1 - core, core)
    for at, apart in enumerate(APART["pack"]):
        here = block // 4 == at + 1
        pack, core = jnp.where(here, pack_me ^ apart, pack), jnp.where(here, 1 - core, core)
    return chip, core, pack


def body(images, captions, caption_owner, caption_count, log_scale, bias):
    pair_rows, width = images.shape
    slots = captions.shape[0]
    packers = lax.axis_size("pack")
    chips = lax.axis_size("chip")
    assert pair_rows + slots < ROWS and slots <= 128 and pair_rows * packers <= 256
    assert chips * packers % CHUNK == 0
    vmem = pl.BlockSpec(memory_space=pltpu.VMEM)
    smem = pl.BlockSpec(memory_space=pltpu.SMEM)
    sent, own, aside = pl.pallas_call(
        pack_kernel,
        out_shape=(
            pltpu.VMEM((ROWS, width), jnp.bfloat16),
            pltpu.VMEM((ROWS, width), jnp.float32),
            pltpu.VMEM((ROWS, 128), jnp.float32),
        ),
        in_specs=[vmem, vmem, vmem, smem],
        out_specs=(vmem, vmem, vmem),
    )(images, captions, caption_owner, caption_count)
    mine = gather(sent)
    other = lax.ppermute(mine, "core", [(0, 1), (1, 0)])
    row_loss, grad_images, grad_captions = pl.pallas_call(
        functools.partial(pair_kernel, chips, packers, pair_rows, slots),
        out_shape=(
            jax.ShapeDtypeStruct((1, pair_rows), jnp.float32),
            jax.ShapeDtypeStruct(images.shape, jnp.float32),
            jax.ShapeDtypeStruct(captions.shape, jnp.float32),
        ),
        in_specs=[smem] * 2 + [vmem] * 4,
        out_specs=(vmem, vmem, vmem),
        compiler_params=pltpu.CompilerParams(vmem_limit_bytes=32 * 1024 * 1024),
    )(log_scale, bias, own, aside, mine, other)
    return row_loss.reshape(pair_rows), grad_images, grad_captions


def solution(mesh):
    cycles, packers = mesh.devices.shape
    split = Mesh(mesh.devices.reshape(cycles // 2, 2, packers), ("chip", "core", "pack"))
    rows = P(("chip", "core", "pack"))
    return jax.shard_map(
        body,
        mesh=split,
        in_specs=(rows, rows, rows, rows, P(), P()),
        out_specs=(rows, rows, rows),
        check_vma=False,
    )
```

```python
import functools

import jax
import jax.numpy as jnp
from jax import lax
from jax.experimental import pallas as pl
from jax.experimental.pallas import tpu as pltpu
from jax.sharding import Mesh
from jax.sharding import PartitionSpec as P

eps = 1e-06
ROWS, SLOTS, PAIR_ROWS = 8, 4, 2
HEAD, TAIL, PIECE = 896, 256, 640
CODES = TAIL + HEAD + TAIL - PIECE
CHUNK = 16
APART = {"chip": (2, 3, 1), "pack": (3, 2, 1)}


def unit_rows(rows):
    floats = rows.astype(jnp.float32)
    inverse = lax.rsqrt(jnp.sum(floats * floats, axis=-1, keepdims=True) + eps)
    return floats * inverse, inverse


def pack_kernel(images_ref, captions_ref, owner_ref, count_ref, sent_ref, own_ref, left_ref, aside_ref):
    pair_rows = images_ref.shape[0]
    slots, width = captions_ref.shape
    owner = owner_ref[...].reshape(1, slots).astype(jnp.float32)
    count = count_ref[0]
    left = ROWS - pair_rows - slots
    images, images_inv = unit_rows(images_ref[...])
    captions, captions_inv = unit_rows(captions_ref[...])
    codes = [jnp.where(slot < count, owner[:, slot : slot + 1], -1.0) for slot in range(slots)]
    own = jnp.concatenate([images, captions, jnp.zeros((left, width), jnp.float32)], axis=0)
    own_ref[...] = own
    own_inv = jnp.concatenate([images_inv, captions_inv, jnp.zeros((left, 1), jnp.float32)], axis=0)
    rows = lax.broadcasted_iota(jnp.int32, (ROWS, 128), 0)
    lanes = lax.broadcasted_iota(jnp.int32, (ROWS, 128), 1)
    aside = jnp.where(lanes == 0, own_inv, 0.0)
    for slot in range(slots):
        aside = jnp.where(jnp.logical_and(lanes == 1, rows == pair_rows + slot), codes[slot], aside)
    aside_ref[...] = aside
    is_image = lax.broadcasted_iota(jnp.int32, (ROWS, 1), 0) < pair_rows

    def blank(lanes_left):
        return jnp.zeros((ROWS, lanes_left), jnp.float32)

    first = jnp.where(is_image, own[:, :HEAD], jnp.concatenate([blank(TAIL), own[:, :PIECE]], axis=1))
    second = jnp.where(
        is_image,
        jnp.concatenate([own[:, HEAD:], blank(HEAD - TAIL)], axis=1),
        jnp.concatenate([blank(TAIL), own[:, PIECE:], blank(HEAD - CODES)], axis=1),
    )
    left_ref[...] = jnp.concatenate([first, second], axis=0).astype(jnp.bfloat16)
    code_lane = lax.broadcasted_iota(jnp.int32, (1, HEAD - CODES), 1)
    code_row = jnp.zeros((1, HEAD - CODES), jnp.float32)
    for slot in range(slots):
        code_row = jnp.where(code_lane == slot, codes[slot], code_row)
    pieces = [
        images[0:1, :PIECE],
        jnp.concatenate([images[0:1, PIECE:], code_row], axis=1),
        images[1:2, :PIECE],
        jnp.concatenate([images[1:2, PIECE:], jnp.zeros_like(code_row)], axis=1),
    ]
    lower = jnp.concatenate([captions[:, HEAD:], jnp.concatenate(pieces, axis=0)], axis=1)
    sent_ref[...] = jnp.concatenate([captions[:, :HEAD], lower], axis=0).astype(jnp.bfloat16)


def scalars_kernel(scale_ref, bias_ref, sent_ref, near_ref, scalars_ref):
    near_ref[...] = sent_ref[...]
    lanes = lax.broadcasted_iota(jnp.int32, (ROWS, 128), 1)
    scale = jnp.exp(jnp.full((ROWS, 128), scale_ref[0], jnp.float32))
    scalars_ref[...] = jnp.where(lanes == 0, scale, bias_ref[0])


def pair_kernel(chips, packers, pair_rows, slots, last, *refs):
    if last:
        left_ref, aside_ref, scalars_ref, rows_ref, own_ref, loss_in_ref, upstream_in_ref = refs[:7]
        loss_ref, grad_images_ref, grad_captions_ref = refs[7:]
    else:
        left_ref, aside_ref, scalars_ref, rows_ref, loss_out_ref, upstream_out_ref = refs
    group_rows = pair_rows * packers
    chip_me, core_me, pack_me = lax.axis_index("chip"), lax.axis_index("core"), lax.axis_index("pack")
    cycle_me = chip_me * 2 + core_me
    me = cycle_me * packers + pack_me
    devices = chips * 2 * packers
    chunk_rows = CHUNK * ROWS

    left = left_ref[...]
    aside = aside_ref[...]
    own_inv, own_codes = aside[:, 0:1], aside[:, 1:2].astype(jnp.int32)
    logit_scale, logit_shift = scalars_ref[:, 0:1], scalars_ref[:, 1:2]

    own_at = lax.broadcasted_iota(jnp.int32, (ROWS, 1), 0)
    own_is_image = own_at < pair_rows
    own_is_slot = jnp.logical_and(own_at >= pair_rows, own_at < pair_rows + slots)
    own_pair = jnp.where(
        own_is_image,
        me * pair_rows + own_at,
        jnp.where(jnp.logical_and(own_is_slot, own_codes >= 0), cycle_me * group_rows + own_codes, -1),
    )

    column = lax.broadcasted_iota(jnp.int32, (1, chunk_rows), 1)
    column_at = column % ROWS
    column_is_image = jnp.logical_or(column_at == SLOTS, column_at == SLOTS + 2)
    column_is_slot = column_at < SLOTS
    lanes_left = HEAD - CODES
    spread = (
        lax.broadcasted_iota(jnp.int32, (lanes_left, chunk_rows), 0)
        == lax.broadcasted_iota(jnp.int32, (lanes_left, chunk_rows), 1) % ROWS
    ).astype(jnp.bfloat16)
    code_row = lax.broadcasted_iota(jnp.int32, (chunk_rows, chunk_rows), 0)
    code_column = lax.broadcasted_iota(jnp.int32, (chunk_rows, chunk_rows), 1)
    code_here = code_row == code_column // ROWS * ROWS + SLOTS + 1

    def one_chunk(rows_ref, core_from, chunk, totals):
        loss, upstream = totals
        rows = rows_ref[pl.ds(chunk * chunk_rows, chunk_rows), :]
        codes = jnp.dot(rows[:, CODES:], spread, preferred_element_type=jnp.float32)
        codes = jnp.sum(jnp.where(code_here, codes, 0.0), axis=0, keepdims=True).astype(jnp.int32)
        block = chunk * CHUNK + column // ROWS
        chip_at, core_at, pack_at = source(block, chip_me, core_from, pack_me, chips, packers)
        cycle_at = chip_at * 2 + core_at
        device = cycle_at * packers + pack_at
        column_pair = jnp.where(
            column_is_image,
            device * pair_rows + (column_at - SLOTS) // 2,
            jnp.where(
                jnp.logical_and(column_is_slot, codes >= 0), cycle_at * group_rows + codes, -1
            ),
        )
        live = jnp.logical_and(
            jnp.logical_and(own_pair >= 0, column_pair >= 0), own_is_image != column_is_image
        )
        products = lax.dot_general(
            left, rows, (((1,), (1,)), ((), ())), preferred_element_type=jnp.float32
        )
        second = products[ROWS:]
        second = jnp.where(
            own_is_image, pltpu.roll(second, chunk_rows - SLOTS, 1), pltpu.roll(second, chunk_rows - 1, 1)
        )
        logits = logit_scale * (products[:ROWS] + second) + logit_shift
        signed = jnp.where(own_pair == column_pair, -logits, logits)
        small = jnp.exp(-jnp.abs(signed))
        softplus = jnp.maximum(signed, 0.0) + jnp.log1p(small)
        sigmoid = jnp.where(signed >= 0.0, 1.0, small) / (1.0 + small)
        loss = loss + jnp.sum(jnp.where(live, softplus, 0.0), axis=1, keepdims=True)
        weights = jnp.where(own_pair == column_pair, -sigmoid, sigmoid)
        weights = jnp.where(live, weights, 0.0)
        second = jnp.where(own_is_image, pltpu.roll(weights, SLOTS, 1), pltpu.roll(weights, 1, 1))
        weights = jnp.concatenate([weights, second], axis=0).astype(jnp.bfloat16)
        upstream = upstream + jnp.dot(weights, rows, preferred_element_type=jnp.float32)
        return loss, upstream

    if last:
        totals = (loss_in_ref[:, 0:1], upstream_in_ref[...])
    else:
        totals = (jnp.zeros((ROWS, 1), jnp.float32), jnp.zeros((2 * ROWS, HEAD), jnp.float32))
    work = functools.partial(one_chunk, rows_ref, 1 - core_me if last else core_me)
    chunks = devices // 2 // CHUNK
    loss, upstream = work(0, totals) if chunks == 1 else lax.fori_loop(0, chunks, work, totals)
    if not last:
        loss_out_ref[...] = jnp.broadcast_to(loss, (ROWS, 128))
        upstream_out_ref[...] = upstream
        return

    own = own_ref[...]
    first, second = upstream[:ROWS], upstream[ROWS:]
    upstream = logit_scale * jnp.where(
        own_is_image,
        jnp.concatenate([first, second[:, :TAIL]], axis=1),
        jnp.concatenate([first[:, TAIL:], second[:, TAIL:CODES]], axis=1),
    )
    grads = own_inv * (upstream - own * jnp.sum(own * upstream, axis=-1, keepdims=True))
    loss = loss / (devices * pair_rows)
    lanes = lax.broadcasted_iota(jnp.int32, (1, pair_rows), 1)
    losses = jnp.zeros((1, pair_rows), jnp.float32)
    for row in range(pair_rows):
        losses = jnp.where(lanes == row, loss[row : row + 1, :], losses)
    loss_ref[...] = losses
    grad_images_ref[...] = grads[:pair_rows]
    grad_captions_ref[...] = jnp.where(own_pair >= 0, grads, 0.0)[pair_rows : pair_rows + slots]


def gather(rows, near):
    chips, packers = lax.axis_size("chip"), lax.axis_size("pack")
    if chips != 4 or packers != 4:
        return lax.all_gather(lax.all_gather(rows, "chip", axis=0, tiled=True), "pack", axis=0, tiled=True)
    for axis, distances in APART.items():
        taken = [near if axis == "chip" else rows]
        for apart in distances:
            pairs = []
            for chip in range(4):
                for core in range(2):
                    for pack in range(4):
                        peer_chip = chip ^ apart if axis == "chip" else chip
                        peer_pack = pack ^ apart if axis == "pack" else pack
                        peer = (peer_chip * 2 + 1 - core) * 4 + peer_pack
                        pairs.append(((chip * 2 + core) * 4 + pack, peer))
            taken.append(lax.ppermute(rows, ("chip", "core", "pack"), pairs))
        rows = jnp.concatenate(taken, axis=0)
    return rows


def source(block, chip_me, core_me, pack_me, chips, packers):
    if chips != 4 or packers != 4:
        return block % chips, core_me, block // chips
    chip, core, pack = chip_me, core_me, pack_me
    for at, apart in enumerate(APART["chip"]):
        here = block % 4 == at + 1
        chip, core = jnp.where(here, chip_me ^ apart, chip), jnp.where(here, 1 - core, core)
    for at, apart in enumerate(APART["pack"]):
        here = block // 4 == at + 1
        pack, core = jnp.where(here, pack_me ^ apart, pack), jnp.where(here, 1 - core, core)
    return chip, core, pack


def body(images, captions, caption_owner, caption_count, log_scale, bias):
    pair_rows, width = images.shape
    slots = captions.shape[0]
    packers = lax.axis_size("pack")
    chips = lax.axis_size("chip")
    assert (pair_rows, slots, width) == (PAIR_ROWS, SLOTS, HEAD + TAIL) and pair_rows * packers <= 256
    assert chips * packers % CHUNK == 0
    vmem = pl.BlockSpec(memory_space=pltpu.VMEM)
    smem = pl.BlockSpec(memory_space=pltpu.SMEM)
    sent, own, left, aside = pl.pallas_call(
        pack_kernel,
        out_shape=(
            pltpu.VMEM((ROWS, HEAD), jnp.bfloat16),
            pltpu.VMEM((ROWS, width), jnp.float32),
            pltpu.VMEM((2 * ROWS, HEAD), jnp.bfloat16),
            pltpu.VMEM((ROWS, 128), jnp.float32),
        ),
        in_specs=[vmem, vmem, vmem, smem],
        out_specs=(vmem, vmem, vmem, vmem),
    )(images, captions, caption_owner, caption_count)
    near, scalars = pl.pallas_call(
        scalars_kernel,
        out_shape=(pltpu.VMEM((ROWS, HEAD), jnp.bfloat16), pltpu.VMEM((ROWS, 128), jnp.float32)),
        in_specs=[smem, smem, vmem],
        out_specs=(vmem, vmem),
    )(log_scale, bias, sent)
    mine = gather(sent, near)
    other = lax.ppermute(mine, "core", [(0, 1), (1, 0)])
    limits = pltpu.CompilerParams(vmem_limit_bytes=32 * 1024 * 1024)
    kernel = functools.partial(pair_kernel, chips, packers, pair_rows, slots)
    loss, upstream = pl.pallas_call(
        functools.partial(kernel, False),
        out_shape=(pltpu.VMEM((ROWS, 128), jnp.float32), pltpu.VMEM((2 * ROWS, HEAD), jnp.float32)),
        in_specs=[vmem] * 4,
        out_specs=(vmem, vmem),
        compiler_params=limits,
        cost_estimate=pl.CostEstimate(flops=64 * HEAD * mine.shape[0], bytes_accessed=2 * mine.size, transcendentals=0),
    )(left, aside, scalars, mine)
    row_loss, grad_images, grad_captions = pl.pallas_call(
        functools.partial(kernel, True),
        out_shape=(
            jax.ShapeDtypeStruct((1, pair_rows), jnp.float32),
            jax.ShapeDtypeStruct(images.shape, jnp.float32),
            jax.ShapeDtypeStruct(captions.shape, jnp.float32),
        ),
        in_specs=[vmem] * 7,
        out_specs=(vmem, vmem, vmem),
        compiler_params=limits,
    )(left, aside, scalars, other, own, loss, upstream)
    return row_loss.reshape(pair_rows), grad_images, grad_captions


def solution(mesh):
    cycles, packers = mesh.devices.shape
    split = Mesh(mesh.devices.reshape(cycles // 2, 2, packers), ("chip", "core", "pack"))
    rows = P(("chip", "core", "pack"))
    return jax.shard_map(
        body,
        mesh=split,
        in_specs=(rows, rows, rows, rows, P(), P()),
        out_specs=(rows, rows, rows),
        check_vma=False,
    )
```
